32 devices in a mesh: dp: 4 (over y, x), ctx: 4 (over z), head: 2 (over core).
Axes of the slice: x: 2, y: 2, z: 4, core: 2. Of those that a mesh axis runs over, the one named last changes fastest.
Arguments:
- tokens: bfloat16 [8, 1024, 1024], P('dp', 'ctx'), may hold values from -6 to 6
- segments: int32 [8, 1024], P('dp', 'ctx'), may hold values from 0 to 5, as said below
- cotangent: bfloat16 [8, 1024, 1024], P('dp', 'ctx'), may hold values from -6 to 6
- inner_proj: bfloat16 [2, 1024, 2, 2048], P(None, ('dp', 'ctx'), None, 'head'), may hold values from -0.1875 to 0.1875
- state_proj: bfloat16 [2, 1024, 256], P(None, ('dp', 'ctx')), may hold values from -0.1875 to 0.1875
- step_proj: bfloat16 [2, 1024, 32], P(None, ('dp', 'ctx'), 'head'), may hold values from -0.1875 to 0.1875
- out_proj: bfloat16 [2, 2048, 1024], P(None, 'head', ('dp', 'ctx')), may hold values from -0.125 to 0.125
- norm_gain: float32 [2, 1024], replicated, may hold values from 0.5 to 1.5
- mix_kernel: float32 [2, 4, 2048], P(None, None, 'head'), may hold values from -3 to 3
- mix_bias: float32 [2, 2048], P(None, 'head'), may hold values from -3 to 3
- state_kernel: float32 [2, 4, 256], replicated, may hold values from -3 to 3
- state_bias: float32 [2, 256], replicated, may hold values from -3 to 3
- step_bias: float32 [2, 32], P(None, 'head'), may hold values from -4 to -2
- decay_log: float32 [2, 32], P(None, 'head'), may hold values from -12 to 1
- skip_gain: float32 [2, 32], P(None, 'head'), may hold values from 0.5 to 1.5
- gate_gain: float32 [2, 2048], P(None, 'head'), may hold values from 0.5 to 1.5
Outputs:
- mixed: bfloat16 [8, 1024, 1024], P('dp', 'ctx')
- token_grad: bfloat16 [8, 1024, 1024], P('dp', 'ctx')
- grad_inner_proj: float32 [2, 1024, 2, 2048], P(None, ('dp', 'ctx'), None, 'head')
- grad_state_proj: float32 [2, 1024, 256], P(None, ('dp', 'ctx'))
- grad_step_proj: float32 [2, 1024, 32], P(None, ('dp', 'ctx'), 'head')
- grad_out_proj: float32 [2, 2048, 1024], P(None, 'head', ('dp', 'ctx'))
- grad_norm_gain: float32 [2, 1024], replicated
- grad_mix_kernel: float32 [2, 4, 2048], P(None, None, 'head')
- grad_mix_bias: float32 [2, 2048], P(None, 'head')
- grad_state_kernel: float32 [2, 4, 256], replicated
- grad_state_bias: float32 [2, 256], replicated
- grad_step_bias: float32 [2, 32], P(None, 'head')
- grad_decay_log: float32 [2, 32], P(None, 'head')
- grad_skip_gain: float32 [2, 32], P(None, 'head')
- grad_gate_gain: float32 [2, 2048], P(None, 'head')
The draws below stay inside these ranges and needn't reach their ends.
Inputs may be any that keep to these rules, and one draw needn't show every extreme that they name: `segments`: in each sequence the numbers start at 0 and rise by one where a document begins; a document has 200 to 2000 tokens, except the last of a sequence, which may be shorter, and except a document that makes up a whole sequence, which has all of its tokens; in each group of 2 consecutive sequences at least one is a single document.
All inputs are finite; a program needn't handle non-finite values.
Results may differ from the reference program's by a relative error of at most 0.02.
Values may be sent and summed in bfloat16 or wider, within the bound.
No kernel may reach another device: no remote copies, remote signals or barrier semaphores. Data moves between devices by JAX's collectives and lax.ppermute only.
A program may use at most 256 MiB of HBM per device.

```python
import jax
import jax.numpy as jnp
from jax import lax

D = 1024
DI = 2048
H = 32
HEADDIM = 64
DSTATE = 128
CONV = 4
BLOCK = 256
LAYERS = 2
SEQS = 2
DOC_MIN = 200
DOC_MAX = 2000
LENGTH = 1024
BATCH = 8


def head_rates(key, slow_share):
    pick_key, slow_key, fast_key, step_key = jax.random.split(key, 4)
    shape = (LAYERS, H)
    slow = jax.random.uniform(pick_key, shape) < slow_share
    slow_rate = jnp.exp(jax.random.uniform(slow_key, shape, minval=jnp.log(0.02 / LENGTH), maxval=jnp.log(0.5 / LENGTH)))
    fast_rate = jnp.exp(jax.random.uniform(fast_key, shape, minval=jnp.log(0.015), maxval=jnp.log(0.05)))
    rate = jnp.where(slow, slow_rate, fast_rate)
    delta = jnp.exp(jax.random.uniform(step_key, shape, minval=jnp.log(0.02), maxval=jnp.log(0.1)))
    return (rate, delta)


def draw_step_bias(key, part):
    rate, delta = head_rates(key, 0.5)
    return jnp.log(jnp.expm1(delta)).astype(jnp.float32)


def draw_decay_log(key, part):
    rate, delta = head_rates(key, 0.5)
    return jnp.log(rate / delta).astype(jnp.float32)


def draw_segments(key, part):
    key = jax.random.fold_in(key, 11)
    size_key, whole_key = jax.random.split(key)
    slots = LENGTH // DOC_MIN + 1
    sizes = jax.random.randint(size_key, (BATCH, slots), DOC_MIN, DOC_MAX + 1)
    groups = BATCH // SEQS
    pick = jax.random.randint(whole_key, (groups,), 0, SEQS)
    rows = jnp.arange(BATCH)
    dense = rows == (pick[0] + 1) % SEQS
    sizes = jnp.where(dense[:, None], DOC_MIN, sizes)
    ends = jnp.cumsum(sizes, axis=1)
    position = jnp.arange(LENGTH)
    numbers = jnp.sum((ends[:, None, :] <= position[None, :, None]).astype(jnp.int32), axis=2)
    whole = rows % SEQS == jnp.repeat(pick, SEQS)
    return jnp.where(whole[:, None], 0, numbers).astype(jnp.int32)


def shard_levels(stream_key, shape, cuts, least, high):
    level, own = 1.0, jax.random.fold_in(stream_key, 6)
    for dim, shards_of in cuts:
        draws = jnp.exp(jax.random.uniform(jax.random.fold_in(own, dim), (shards_of,), jnp.float32, least / len(cuts), high / len(cuts)))
        level = level * jnp.repeat(draws, shape[dim] // shards_of).reshape([-1 if axis == dim else 1 for axis in range(len(shape))])
    return level


def gaussian(key, extent, spread, bound, cuts=(), kind=jnp.bfloat16):
    values = jax.random.normal(key, extent, jnp.float32) * spread
    if len(cuts) > 0:
        values = shard_levels(key, extent, cuts, -0.22, 0.18) * values
    return jnp.clip(values, min=-bound, max=bound).astype(kind)


def setup_inputs(seed: int = 0) -> dict:
    arg_keys = jax.random.split(jax.random.key(seed), 17)
    return {
        "tokens": gaussian(arg_keys[0], (BATCH, LENGTH, D), 1.0, 6.0, ((0, 4), (1, 4))),
        "segments": draw_segments(jax.random.fold_in(arg_keys[16], 71), 0),
        "cotangent": gaussian(arg_keys[2], (BATCH, LENGTH, D), 1.0, 6.0, ((0, 4), (1, 4))),
        "inner_proj": gaussian(arg_keys[3], (LAYERS, D, 2, DI), D ** -0.5, 0.1875, ((1, 16), (3, 2))),
        "state_proj": gaussian(arg_keys[4], (LAYERS, D, 2 * DSTATE), D ** -0.5, 0.1875, ((1, 16),)),
        "step_proj": gaussian(arg_keys[5], (LAYERS, D, H), D ** -0.5, 0.1875, ((1, 16), (2, 2))),
        "out_proj": gaussian(arg_keys[6], (LAYERS, DI, D), DI ** -0.5, 0.125, ((1, 2), (2, 16))),
        "norm_gain": jnp.clip(1.0 + 0.1 * jax.random.normal(arg_keys[7], (LAYERS, D), jnp.float32), 0.5, 1.5),
        "mix_kernel": gaussian(arg_keys[8], (LAYERS, CONV, DI), CONV ** -0.5, 3.0, ((2, 2),), jnp.float32),
        "mix_bias": gaussian(arg_keys[9], (LAYERS, DI), 0.5, 3.0, ((1, 2),), jnp.float32),
        "state_kernel": gaussian(arg_keys[10], (LAYERS, CONV, 2 * DSTATE), CONV ** -0.5, 3.0, (), jnp.float32),
        "state_bias": gaussian(arg_keys[11], (LAYERS, 2 * DSTATE), 0.5, 3.0, (), jnp.float32),
        "step_bias": draw_step_bias(jax.random.fold_in(arg_keys[16], 71), 0),
        "decay_log": draw_decay_log(jax.random.fold_in(arg_keys[16], 71), 0),
        "skip_gain": jnp.clip(0.5 + 1.0 * jax.random.uniform(arg_keys[14], (LAYERS, H), jnp.float32) ** shard_levels(arg_keys[14], (LAYERS, H), ((1, 2),), -0.2, 0.2), 0.5, 1.5),
        "gate_gain": jnp.clip(1.0 + 0.1 * jax.random.normal(arg_keys[15], (LAYERS, DI), jnp.float32), 0.5, 1.5),
    }


EPSILON = 1e-05
HIGH = lax.Precision.HIGHEST

@jax.custom_vjp
def low(v):
    return lax.optimization_barrier(v.astype(jnp.bfloat16)).astype(jnp.float32)

@jax.custom_vjp
def low_back(v):
    return v

def low_keep(v):
    return (low(v), None)

def low_pass(kept, grad):
    return (grad,)

def back_keep(v):
    return (v, None)

def back_low(kept, grad):
    return (low(grad),)
low.defvjp(low_keep, low_pass)
low_back.defvjp(back_keep, back_low)

def scaled_norm(residual, gain):
    return residual * lax.rsqrt(lax.optimization_barrier(jnp.mean(residual * residual, axis=-1, keepdims=True)) + EPSILON) * gain

def conv_act(window, weight, bias, labels, segment):
    count = segment.shape[-1]
    total = bias
    for offset in range(weight.shape[0]):
        match = (labels[..., offset:offset + count] == segment).astype(jnp.float32)[..., None]
        total = total + weight[offset] * window[..., offset:offset + count, :] * match
    return jax.nn.silu(total)

def block_local(inner, bstate, cstate, steps_raw, step_bias, decay_log, skip_gain, segment, before):
    count = segment.shape[0]
    delta = jax.nn.softplus(steps_raw + step_bias)
    accrued = jnp.cumsum(-delta * jnp.exp(decay_log), axis=0)
    order = jnp.arange(count)
    same = (segment[:, None] == segment[None, :]) & (order[:, None] >= order[None, :])
    within = jnp.where(same[:, :, None], accrued[:, None, :] - accrued[None, :, :], 0.0)
    decay = jnp.exp(within) * same.astype(jnp.float32)[:, :, None]
    gram = jnp.dot(cstate, bstate.T, precision=HIGH)
    scaled = inner * delta[:, :, None]
    output = jnp.einsum('tsh,shp->thp', gram[:, :, None] * decay, scaled, precision=HIGH) + skip_gain[None, :, None] * inner
    entry = jnp.exp(accrued) * (segment == before).astype(jnp.float32)[:, None]
    tail = jnp.exp(accrued[-1][None, :] - accrued) * (segment == segment[-1]).astype(jnp.float32)[:, None]
    local = jnp.einsum('sh,shp,sn->hpn', tail, scaled, bstate, precision=HIGH)
    carry = jnp.exp(accrued[-1]) * (segment[-1] == before).astype(jnp.float32)
    return (output, entry, local, carry)

def layer(residual, segment, params):
    inner_proj, state_proj, step_proj, out_proj, norm_gain, mix_kernel, mix_bias, state_kernel, state_bias, step_bias, decay_log, skip_gain, gate_gain = params
    length = residual.shape[0]
    normed = low(scaled_norm(residual, norm_gain))
    both = jnp.einsum('ld,dkc->lkc', normed, inner_proj, precision=HIGH)
    gate = low_back(both[:, 0])
    inner_raw = low_back(low(both[:, 1]))
    state_raw = low_back(low(jnp.dot(normed, state_proj, precision=HIGH)))
    steps_raw = low_back(jnp.dot(normed, step_proj, precision=HIGH))
    stack = jnp.concatenate([inner_raw, state_raw], axis=1)
    window = jnp.concatenate([jnp.zeros((CONV - 1, stack.shape[1]), jnp.float32), stack], axis=0)
    labels = jnp.concatenate([jnp.zeros((CONV - 1,), jnp.int32), segment])
    weight = jnp.concatenate([mix_kernel, state_kernel], axis=1)
    bias = jnp.concatenate([mix_bias, state_bias])
    active = low(conv_act(window, weight, bias, labels, segment))
    inner = active[:, :DI].reshape(length, H, HEADDIM)
    bstate = active[:, DI:DI + DSTATE]
    cstate = active[:, DI + DSTATE:]
    blocks = length // BLOCK
    before = jnp.concatenate([jnp.zeros((1,), jnp.int32), segment[BLOCK - 1:length - 1:BLOCK]])

    def advance(carried, piece):
        output, entry, local, carry = block_local(piece[0], piece[1], piece[2], piece[3], step_bias, decay_log, skip_gain, piece[4], piece[5])
        reach = jnp.einsum('tn,hpn->thp', piece[2], carried, precision=HIGH)
        return (carry[:, None, None] * carried + local, output + entry[:, :, None] * reach)
    pieces = (inner.reshape(blocks, BLOCK, H, HEADDIM), bstate.reshape(blocks, BLOCK, DSTATE), cstate.reshape(blocks, BLOCK, DSTATE), steps_raw.reshape(blocks, BLOCK, H), segment.reshape(blocks, BLOCK), before)
    start = jnp.zeros((H, HEADDIM, DSTATE), jnp.float32)
    _, mixer = lax.scan(jax.checkpoint(advance), start, pieces)
    gated = mixer.reshape(length, DI) * jax.nn.silu(gate)
    square_mean = lax.optimization_barrier(jnp.sum(gated * gated, axis=-1, keepdims=True)) / DI
    normal = low(gated * lax.rsqrt(square_mean + EPSILON) * gate_gain)
    return residual + low_back(jnp.dot(normal, out_proj, precision=HIGH))

def reference(tokens, segments, cotangent, inner_proj, state_proj, step_proj, out_proj, norm_gain, mix_kernel, mix_bias, state_kernel, state_bias, step_bias, decay_log, skip_gain, gate_gain):
    params = tuple((weight.astype(jnp.float32) for weight in (inner_proj, state_proj, step_proj, out_proj, norm_gain, mix_kernel, mix_bias, state_kernel, state_bias, step_bias, decay_log, skip_gain, gate_gain)))

    def forward(residual, segment, weights):
        for layer_index in range(LAYERS):
            residual = layer(residual, segment, tuple((weight[layer_index] for weight in weights)))
        return residual

    def visit(totals, item):
        first, segment, upstream = item
        result, pull = jax.vjp(lambda start, weights: forward(start, segment, weights), first, params)
        back_first, back_weights = pull(upstream)
        totals = jax.tree.map(jnp.add, totals, back_weights)
        return (totals, (result.astype(jnp.bfloat16), back_first.astype(jnp.bfloat16)))
    zeros = jax.tree.map(jnp.zeros_like, params)
    totals, (mixed, token_grad) = lax.scan(visit, zeros, (tokens.astype(jnp.float32), segments, cotangent.astype(jnp.float32)))
    return (mixed, token_grad, totals[0], totals[1], totals[2], totals[3], totals[4], totals[5], totals[6], totals[7], totals[8], totals[9], totals[10], totals[11], totals[12])
```

```python
import jax
import jax.numpy as jnp
from jax import lax
from jax.experimental import pallas as pl
from jax.experimental.pallas import tpu as pltpu
from jax.sharding import PartitionSpec as P

EPSILON = 1e-05
F32 = jnp.float32
BF16 = jnp.bfloat16
HIGH = lax.Precision.HIGHEST
CHUNK = 128
LANES = 128
RIM = 8
FAR = -1e30


def mm(a, b, ca=1, cb=0, precision=None):
    return lax.dot_general(
        a, b, (((ca,), (cb,)), ((), ())), precision=precision, preferred_element_type=F32
    )


def split_mm(a, b, ca=1, cb=0):
    top = a.astype(BF16)
    rest = (a - top.astype(F32)).astype(BF16)
    return mm(top, b, ca, cb) + mm(rest, b, ca, cb)


def mm_split(a, b, ca=1, cb=0):
    top = b.astype(BF16)
    rest = (b - top.astype(F32)).astype(BF16)
    return mm(a, top, ca, cb) + mm(a, rest, ca, cb)


def kernel_call(body, outs, scratch, *args):
    return pl.pallas_call(
        body,
        out_shape=outs,
        scratch_shapes=scratch,
        compiler_params=pltpu.CompilerParams(vmem_limit_bytes=48 * 1024 * 1024),
    )(*args)


def grid_masks():
    row = lax.broadcasted_iota(jnp.int32, (CHUNK, CHUNK), 0)
    col = lax.broadcasted_iota(jnp.int32, (CHUNK, CHUNK), 1)
    return row, col


def soft(v):
    return jnp.maximum(v, 0.0) + jnp.log1p(jnp.exp(-jnp.abs(v)))


def sigmoid(v):
    return 1.0 / (1.0 + jnp.exp(-v))


def conv_body(
    raw_ref, halo_ref, traw_ref, info_ref, taps_ref, perhead_ref, spread_ref,
    act_ref, delta_ref, acc_ref, state_ref, total_ref, window,
):
    count, wide = raw_ref.shape
    chunks = count // CHUNK
    width = spread_ref.shape[1]
    row, col = grid_masks()
    tri = (row >= col).astype(F32)
    totals = []
    for c in range(chunks):
        rows = pl.ds(c * CHUNK, CHUNK)
        delta = soft(traw_ref[rows, :] + perhead_ref[0:1, :])
        rate = -delta * jnp.exp(perhead_ref[1:2, :])
        acc = mm(tri, rate, precision=HIGH)
        delta_ref[rows, :] = delta
        acc_ref[rows, :] = acc
        totals.append(acc[CHUNK - 1 : CHUNK, :])
    whole = totals[0]
    for c in range(1, chunks):
        whole = whole + totals[c]
    total_ref[...] = jnp.broadcast_to(
        jnp.exp(whole) * info_ref[count - 1 : count, 6:7], total_ref.shape
    )

    def block(cb, _):
        lanes = pl.ds(pl.multiple_of(cb * LANES, LANES), LANES)
        window[0:RIM, :] = halo_ref[:, lanes].astype(F32)
        window[RIM : RIM + count, :] = raw_ref[:, lanes].astype(F32)
        taps = taps_ref[:, lanes]
        for c in range(chunks):
            base = c * CHUNK
            pre = taps[4:5, :] + taps[3:4, :] * window[RIM + base : RIM + base + CHUNK, :]
            for d in (1, 2, 3):
                moved = window[RIM + base - d : RIM + base - d + CHUNK, :]
                pre = pre + taps[3 - d : 4 - d, :] * (
                    moved * info_ref[base : base + CHUNK, d : d + 1]
                )
            act_ref[base : base + CHUNK, lanes] = (pre * sigmoid(pre)).astype(BF16)
        return 0

    lax.fori_loop(0, wide // LANES, block, 0)
    spread = spread_ref[...]
    state = jnp.zeros((LANES, width), F32)
    after = jnp.zeros_like(totals[0])
    for c in reversed(range(chunks)):
        rows = pl.ds(c * CHUNK, CHUNK)
        weight = (
            jnp.exp(totals[c] - acc_ref[rows, :] + after) * info_ref[rows, 7:8] * delta_ref[rows, :]
        )
        scaled = act_ref[rows, 0:width].astype(F32) * split_mm(weight, spread)
        state = state + mm_split(act_ref[rows, width : width + LANES], scaled, 0, 0)
        after = after + totals[c]
    state_ref[...] = state


def chunk_terms(c, acc_ref, info_ref, segrow_ref):
    rows = pl.ds(pl.multiple_of(c * CHUNK, CHUNK), CHUNK)
    acc = acc_ref[rows, :]
    row, col = grid_masks()
    same = (info_ref[rows, 0:1] == segrow_ref[0:1, rows]) & (row >= col)
    blocked = jnp.where(same, 0.0, FAR)
    total = acc[CHUNK - 1 : CHUNK, :]
    flags = info_ref[rows, :]
    entry = jnp.exp(acc) * flags[:, 4:5]
    tail = jnp.exp(total - acc) * flags[:, 5:6]
    carry = jnp.exp(total) * flags[CHUNK - 1 : CHUNK, 4:5]
    return rows, acc, acc.T, blocked, entry, tail, carry


def mix_body(
    act_ref, delta_ref, acc_ref, info_ref, segrow_ref, perhead_ref, spread_ref, start_ref,
    gate_ref, gain_ref, y_ref, scaled_ref, squares_ref, states_ref, state,
):
    count, width = gate_ref.shape
    spread = spread_ref[...]
    state[...] = start_ref[...].astype(F32)
    skip = split_mm(perhead_ref[...], spread)[2:3, :]
    lane = lax.broadcasted_iota(jnp.int32, (CHUNK, LANES), 1)
    low_half = lane < LANES // 2

    def step(c, _):
        rows, acc, across, blocked, entry, tail, carry = chunk_terms(
            c, acc_ref, info_ref, segrow_ref
        )
        now = state[...]
        now_low = now.astype(BF16)
        states_ref[pl.ds(pl.multiple_of(c * LANES, LANES), LANES), :] = now_low
        bstate = act_ref[rows, width : width + LANES]
        cstate = act_ref[rows, width + LANES : width + 2 * LANES]
        gram = mm(cstate, bstate, 1, 1)
        x = act_ref[rows, 0:width].astype(F32)
        scaled = x * split_mm(delta_ref[rows, :], spread)
        z = scaled.astype(BF16)
        y_ref[rows, :] = split_mm(entry, spread) * mm_split(cstate, now) + skip * x
        tailed = scaled * split_mm(tail, spread)
        state[...] = split_mm(carry, spread) * now + mm_split(bstate, tailed, 0, 0)
        squares = jnp.zeros((CHUNK, LANES), F32)
        for pair in range(width // LANES):
            lanes = slice(pair * LANES, (pair + 1) * LANES)
            zb = z[:, lanes]
            out = y_ref[rows, lanes]
            for half in (0, 1):
                h = 2 * pair + half
                decay = jnp.exp(acc[:, h : h + 1] - across[h : h + 1, :] + blocked)
                keep = low_half if half == 0 else jnp.logical_not(low_half)
                zh = jnp.where(keep, zb, jnp.zeros_like(zb))
                zl = (jnp.where(keep, scaled[:, lanes], 0.0) - zh.astype(F32)).astype(BF16)
                mat = gram * decay
                top = mat.astype(BF16)
                rest = (mat - top.astype(F32)).astype(BF16)
                out = out + mm(top, zh) + mm(rest, zh) + mm(top, zl)
            y_ref[rows, lanes] = out
            gate = gate_ref[rows, lanes]
            gated = out * (gate * sigmoid(gate))
            squares = squares + gated * gated
            scaled_ref[rows, lanes] = gated
        squares_ref[rows, :] = jnp.broadcast_to(
            jnp.sum(squares, axis=1, keepdims=True), (CHUNK, LANES)
        )
        return 0

    lax.fori_loop(0, count // CHUNK, step, 0)


def gate_body(
    bn_ref, y_ref, gate_ref, gain_ref, factor_ref, act_ref, acc_ref, info_ref, spread_ref,
    dy_ref, dgate_ref, ggrad_ref, state_ref,
):
    count, width = bn_ref.shape
    chunks = count // CHUNK
    spread = spread_ref[...]
    state = jnp.zeros((LANES, width), F32)
    before = jnp.zeros((1, LANES), F32)
    sums = jnp.zeros((1, width), F32)
    for c in range(chunks):
        rows = slice(c * CHUNK, (c + 1) * CHUNK)
        bn = bn_ref[rows, :]
        y = y_ref[rows, :]
        gate = gate_ref[rows, :]
        root = factor_ref[rows, 0:1]
        coef = factor_ref[rows, 1:2]
        sig = sigmoid(gate)
        silu = gate * sig
        gated = y * silu
        back = root * (bn * gain_ref[0:1, :]) - gated * coef
        dy = back * silu
        dy_ref[rows, :] = dy.astype(BF16)
        dgate_ref[rows, :] = (back * y * (sig * (1.0 + gate * (1.0 - sig)))).astype(BF16)
        sums = sums + jnp.sum(bn * gated * root, axis=0, keepdims=True)
        acc = acc_ref[rows, :]
        entry = jnp.exp(acc + before) * info_ref[rows, 6:7]
        cstate = act_ref[rows, width + LANES : width + 2 * LANES]
        state = state + mm(cstate, (dy * split_mm(entry, spread)).astype(BF16), 0, 0)
        before = before + acc[CHUNK - 1 : CHUNK, :]
    ggrad_ref[...] = jnp.broadcast_to(sums, ggrad_ref.shape)
    state_ref[...] = state.astype(BF16)


def back_body(
    act_ref, delta_ref, acc_ref, traw_ref, info_ref, segrow_ref, ahead_ref, perhead_ref, spread_ref,
    states_ref, later_ref, dy_ref, raw_ref, halo_ref, taps_ref,
    dv_ref, dvs_ref, rim_ref, last_ref, dtraw_ref, tapgrad_ref, headgrad_ref,
    dstate, dact, window, gradient,
):
    count, wide = raw_ref.shape
    width = spread_ref.shape[1]
    chunks = count // CHUNK
    spread = spread_ref[...]
    dstate[...] = later_ref[...].astype(F32)
    skip = split_mm(perhead_ref[...], spread)[2:3, :]
    row, col = grid_masks()
    upper = (row <= col).astype(F32)
    lower = (row > col).astype(F32)
    upper_low = upper.astype(BF16)
    lane = lax.broadcasted_iota(jnp.int32, (CHUNK, LANES), 1)
    low_half = lane < LANES // 2
    headgrad_ref[...] = jnp.zeros_like(headgrad_ref)
    decay_rate = jnp.exp(perhead_ref[1:2, :])

    def step(index, _):
        c = chunks - 1 - index
        rows, acc, across, blocked, entry, tail, carry = chunk_terms(
            c, acc_ref, info_ref, segrow_ref
        )
        delta = delta_ref[rows, :]
        bstate = act_ref[rows, width : width + LANES]
        cstate = act_ref[rows, width + LANES : width + 2 * LANES]
        gram = mm(cstate, bstate, 1, 1)
        x = act_ref[rows, 0:width].astype(F32)
        dy_low = dy_ref[rows, :]
        dy = dy_low.astype(F32)
        wide_delta = split_mm(delta, spread)
        scaled = x * wide_delta
        z = scaled.astype(BF16)
        later = dstate[...]
        later_low = later.astype(BF16)
        now_low = states_ref[pl.ds(pl.multiple_of(c * LANES, LANES), LANES), :]
        wide_tail = split_mm(tail, spread)
        tail_in = wide_tail * mm(bstate, later_low)
        entered = dy * split_mm(entry, spread)
        entered_low = entered.astype(BF16)
        from_entry = split_mm(entered * mm(cstate, now_low), spread, 1, 1)
        from_tail = split_mm(scaled * tail_in, spread, 1, 1)
        wide_carry = split_mm(carry, spread)
        kept = jnp.sum(later * now_low.astype(F32), axis=0, keepdims=True) * wide_carry
        from_carry = split_mm(jnp.broadcast_to(kept, (8, width)), spread, 1, 1)[0:1, :]
        dstate[...] = wide_carry * later + mm(cstate, entered_low, 0, 0)
        drate = (
            mm(upper, from_entry, precision=HIGH) + mm(lower, from_tail, precision=HIGH) + from_carry
        )
        dgram = jnp.zeros((CHUNK, CHUNK), F32)
        direct = jnp.zeros((CHUNK, LANES), F32)
        for pair in range(width // LANES):
            lanes = slice(pair * LANES, (pair + 1) * LANES)
            zb = z[:, lanes]
            dyb = dy_low[:, lanes]
            back = tail_in[:, lanes]
            for half in (0, 1):
                h = 2 * pair + half
                keep = low_half if half == 0 else jnp.logical_not(low_half)
                dyh = jnp.where(keep, dyb, jnp.zeros_like(dyb))
                decay = jnp.exp(acc[:, h : h + 1] - across[h : h + 1, :] + blocked)
                grad = mm(dyh, zb, 1, 1) * decay
                dgram = dgram + grad
                moved = mm(upper_low, (grad * gram).astype(BF16)) * lower
                drate = drate + jnp.where(lane == h, jnp.sum(moved, axis=1, keepdims=True), 0.0)
                back = back + mm((gram * decay).astype(BF16), dyh, 0, 0)
            direct = direct + split_mm(x[:, lanes] * back, spread[:, lanes], 1, 1)
            dact[rows, lanes] = wide_delta[:, lanes] * back + skip[:, lanes] * dy[:, lanes]
        dgram_low = dgram.astype(BF16)
        tailed = (scaled * wide_tail).astype(BF16)
        dact[rows, width : width + LANES] = mm(dgram_low, cstate, 0, 0) + mm(
            tailed, later_low, 1, 1
        )
        dact[rows, width + LANES : width + 2 * LANES] = mm(dgram_low, bstate) + mm(
            entered_low, now_low, 1, 1
        )
        ddelta = direct - decay_rate * drate
        dtraw = ddelta * sigmoid(traw_ref[rows, :] + perhead_ref[0:1, :])
        dtraw_ref[rows, :] = dtraw.astype(BF16)
        rate = -delta * decay_rate
        skipped = split_mm(x * dy, spread, 1, 1)
        headgrad_ref[0:1, :] += jnp.sum(dtraw, axis=0, keepdims=True)
        headgrad_ref[1:2, :] += jnp.sum(drate * rate, axis=0, keepdims=True)
        headgrad_ref[2:3, :] += jnp.sum(skipped, axis=0, keepdims=True)
        return 0

    lax.fori_loop(0, chunks, step, 0)
    gradient[0:RIM, :] = jnp.zeros((RIM, LANES), F32)
    gradient[RIM + count : 2 * RIM + count, :] = jnp.zeros((RIM, LANES), F32)

    def block(lanes, put):
        window[0:RIM, :] = halo_ref[:, lanes].astype(F32)
        window[RIM : RIM + count, :] = raw_ref[:, lanes].astype(F32)
        taps = taps_ref[:, lanes]
        sums = [jnp.zeros((1, LANES), F32) for _ in range(5)]
        for c in range(chunks):
            base = c * CHUNK
            moved = [window[RIM + base : RIM + base + CHUNK, :]]
            for d in (1, 2, 3):
                moved.append(
                    window[RIM + base - d : RIM + base - d + CHUNK, :]
                    * info_ref[base : base + CHUNK, d : d + 1]
                )
            pre = taps[4:5, :]
            for d in range(4):
                pre = pre + taps[3 - d : 4 - d, :] * moved[d]
            sig = sigmoid(pre)
            dpre = dact[base : base + CHUNK, lanes] * (sig * (1.0 + pre * (1.0 - sig)))
            gradient[RIM + base : RIM + base + CHUNK, :] = dpre
            for d in range(4):
                sums[3 - d] = sums[3 - d] + jnp.sum(dpre * moved[d], axis=0, keepdims=True)
            sums[4] = sums[4] + jnp.sum(dpre, axis=0, keepdims=True)
        for index in range(5):
            tapgrad_ref[index : index + 1, lanes] = sums[index]

        def pulled(base, size):
            out = taps[3:4, :] * gradient[base : base + size, :]
            for d in (1, 2, 3):
                out = out + taps[3 - d : 4 - d, :] * (
                    gradient[base + d : base + d + size, :] * ahead_ref[base : base + size, d : d + 1]
                )
            return out

        put(pulled, lanes)

    def put_x(pulled, lanes):
        rim_ref[:, lanes] = pulled(0, RIM)
        for c in range(chunks):
            back = pulled(RIM + c * CHUNK, CHUNK)
            dv_ref[c * CHUNK : (c + 1) * CHUNK, lanes] = back.astype(BF16)
            if c == chunks - 1:
                last_ref[:, lanes] = back[CHUNK - RIM :, :]

    def put_state(at):
        def put(pulled, lanes):
            dvs_ref[0:RIM, at : at + LANES] = pulled(0, RIM)
            for c in range(chunks):
                base = RIM + c * CHUNK
                dvs_ref[base : base + CHUNK, at : at + LANES] = pulled(base, CHUNK)

        return put

    def loop(cb, _):
        block(pl.ds(pl.multiple_of(cb * LANES, LANES), LANES), put_x)
        return 0

    lax.fori_loop(0, width // LANES, loop, 0)
    for at in range(0, wide - width, LANES):
        block(slice(width + at, width + at + LANES), put_state(at))
    tapgrad_ref[5:8, :] = jnp.zeros((3, wide), F32)


def swap(x, axis, bit):
    size = lax.axis_size(axis)
    return lax.ppermute(x, axis, [(i, i ^ bit) for i in range(size)])


def bits_of(axis):
    size = lax.axis_size(axis)
    return [1 << k for k in reversed(range(size.bit_length() - 1))]


def gather_near(x):
    for bit in bits_of("ctx"):
        x = jnp.concatenate([x, swap(x, "ctx", bit)], axis=0)
    return x


def gather_far(near):
    if lax.axis_size("dp") != 4:
        x = near
        for bit in reversed(bits_of("dp")):
            x = jnp.concatenate([x, swap(x, "dp", bit)], axis=0)
        return x
    half = near.shape[0] // 2
    one = swap(near, "dp", 1)
    two = swap(near, "dp", 2)
    three = [swap(one[:half], "dp", 2), swap(two[half:], "dp", 1)]
    return jnp.concatenate([near, one, two] + three, axis=0)


def scatter_rows(*matrices):
    count = lax.axis_size("dp")
    group = matrices[0].shape[0] // count

    def part(start, size):
        return jnp.concatenate([g[start : start + size] for g in matrices], axis=1)

    if count != 4:
        whole = part(0, count * group).astype(F32)
        for bit in bits_of("dp"):
            size = bit * group
            whole = whole[:size] + swap(whole[size:].astype(BF16), "dp", bit).astype(F32)
        near = whole
    else:
        half = group // 2
        far_one = swap(part(3 * group, half), "dp", 2).astype(F32)
        far_two = swap(part(3 * group + half, half), "dp", 1).astype(F32)
        none = jnp.zeros_like(far_one)
        one = part(group, group).astype(F32) + jnp.concatenate([far_one, none])
        two = part(2 * group, group).astype(F32) + jnp.concatenate([none, far_two])
        near = (
            part(0, group).astype(F32)
            + swap(one.astype(BF16), "dp", 1).astype(F32)
            + swap(two.astype(BF16), "dp", 2).astype(F32)
        )
    for bit in reversed(bits_of("ctx")):
        half = near.shape[0] // 2
        near = near[:half] + swap(near[half:].astype(BF16), "ctx", bit).astype(F32)
    return near


def total_over(x):
    for axis in ("ctx", "dp"):
        for bit in bits_of(axis):
            x = x + swap(x, axis, bit)
    return x


def head_sum(x):
    low = x.astype(BF16)
    return low.astype(F32) + swap(low, "head", 1).astype(F32)


def own_half(x, other=False):
    half = x.shape[-1] // 2
    first = (lax.axis_index("head") == 0) != other
    return jnp.where(first, x[..., :half], x[..., half:])


def both_halves(own, other):
    return jnp.where(
        lax.axis_index("head") == 0,
        jnp.concatenate([own, other], axis=-1),
        jnp.concatenate([other, own], axis=-1),
    )


def to_runs(blocks):
    count, me = lax.axis_size("ctx"), lax.axis_index("ctx")
    even = me % 2 == 0
    first = jnp.where(even, blocks[0], blocks[1])
    second = jnp.where(even, blocks[1], blocks[0])
    half = count // 2
    one = [(2 * j, j) for j in range(half)] + [(2 * j + 1, half + j) for j in range(half)]
    two = [(2 * j + 1, j) for j in range(half)] + [(2 * j, half + j) for j in range(half)]
    got_one = lax.ppermute(first, "ctx", one)
    got_two = lax.ppermute(second, "ctx", two)
    early = me < half
    return jnp.stack([jnp.where(early, got_one, got_two), jnp.where(early, got_two, got_one)])


def from_runs(blocks):
    count, me = lax.axis_size("ctx"), lax.axis_index("ctx")
    half = count // 2
    early = me < half
    one = [(j, 2 * j) for j in range(half)] + [(half + j, 2 * j + 1) for j in range(half)]
    two = [(j, 2 * j + 1) for j in range(half)] + [(half + j, 2 * j) for j in range(half)]
    got_one = lax.ppermute(jnp.where(early, blocks[0], blocks[1]), "ctx", one)
    got_two = lax.ppermute(jnp.where(early, blocks[1], blocks[0]), "ctx", two)
    even = me % 2 == 0
    return jnp.stack([jnp.where(even, got_one, got_two), jnp.where(even, got_two, got_one)])


def shared(move, blocks, extra=None):
    rows = blocks.shape[1] // 2
    mine = lax.axis_index("head")
    send = lax.dynamic_slice_in_dim(blocks, mine * rows, rows, 1)
    if extra is not None:
        send = jnp.concatenate([send, extra], axis=1)
    got = move(send)
    own = got[:, :rows]
    other = swap(own, "head", 1)
    whole = jnp.where(
        mine == 0,
        jnp.concatenate([own, other], axis=1),
        jnp.concatenate([other, own], axis=1),
    )
    return whole if extra is None else (whole, got[:, rows:])


def chain_shift(x, by):
    count = lax.axis_size("ctx")
    half = count // 2
    pairs = [
        (i, i + by) for i in range(count) if 0 <= i + by < count and i // half == (i + by) // half
    ]
    return lax.ppermute(x, "ctx", pairs)


def chain_scan(state, total, back):
    sign = -1 if back else 1
    half = lax.axis_size("ctx") // 2
    state = chain_shift(state, sign)
    if half == 2:
        return state
    total = chain_shift(total, sign)
    state = state.astype(F32)
    by = 1
    while by < half - 1:
        state = state + total * chain_shift(state, sign * by)
        total = total * chain_shift(total, sign * by)
        by *= 2
    return state.astype(BF16)


def shape(rows, cols, kind=F32):
    return jax.ShapeDtypeStruct((rows, cols), kind)


def layer_forward(residual, weights, small, common):
    wx, wstate, wgate, wout = weights
    info, segrow, _, spread = common
    count = residual.shape[0]
    width = spread.shape[1]
    wide = width + 2 * LANES
    root = lax.rsqrt(jnp.mean(residual * residual, axis=-1, keepdims=True) + EPSILON)
    normed = (residual * root * small["norm_gain"]).astype(BF16)
    both = mm(normed, wx)
    sraw = both_halves(both[:, width : width + LANES], mm(normed, wstate)).astype(BF16)
    raw = jnp.concatenate([both[:, :width].astype(BF16), sraw], axis=1)
    traw = both[:, width + LANES :]
    halo = chain_shift(raw[count - RIM :], 1)
    gate = mm(normed, wgate)
    act, delta, acc, state, total = kernel_call(
        conv_body,
        (
            shape(count, wide, BF16),
            shape(count, LANES),
            shape(count, LANES),
            shape(LANES, width),
            shape(8, LANES),
        ),
        [pltpu.VMEM((count + RIM, LANES), F32)],
        raw, halo, traw, info, small["taps"], small["perhead"], spread,
    )
    wide_total = jnp.repeat(total[0:1, : width // 64], 64, axis=1)
    start = chain_scan(state, wide_total, False)
    y, gated, squares, states = kernel_call(
        mix_body,
        (
            shape(count, width),
            shape(count, width),
            shape(count, LANES),
            shape(count, width, BF16),
        ),
        [pltpu.VMEM((LANES, width), F32)],
        act, delta, acc, info, segrow, small["perhead"], spread, start, gate, small["gate_gain"],
    )
    own = squares[:, 0:1]
    channels = width * lax.axis_size("head")
    out_root = lax.rsqrt((own + swap(own, "head", 1)) / channels + EPSILON)
    normal = (gated * out_root * small["gate_gain"][0:1]).astype(BF16)
    branch = mm(normal, wout, 1, 1)
    branch = branch + swap(branch, "head", 1)
    kept = (residual, root, normed, raw, traw, halo, gate, act, delta, acc, wide_total, y, normal)
    return residual + branch, kept + (states, out_root, branch)


def layer_backward(upstream, weights, small, common, kept):
    wx, _, wgate, wout = weights
    info, segrow, ahead, spread = common
    (
        residual, root, normed, raw, traw, halo, gate, act, delta, acc, wide_total, y, normal,
        states, out_root, branch,
    ) = kept
    count = residual.shape[0]
    width = spread.shape[1]
    wide = width + 2 * LANES
    channels = width * lax.axis_size("head")
    wire = upstream.astype(BF16)
    bn = mm(wire, wout)
    dot = jnp.sum(wire.astype(F32) * branch, axis=-1, keepdims=True)
    factor = jnp.concatenate(
        [out_root, out_root**2 * dot / channels, jnp.zeros((count, LANES - 2), F32)], axis=1
    )
    dy, dgate, gate_grad, local = kernel_call(
        gate_body,
        (
            shape(count, width, BF16),
            shape(count, width, BF16),
            shape(8, width),
            shape(LANES, width, BF16),
        ),
        [],
        bn, y, gate, small["gate_gain"], factor, act, acc, info, spread,
    )
    later = chain_scan(local, wide_total, True)
    out_grad = mm(wire, normal, 0, 0).astype(BF16)
    gate_w_grad = mm(normed, dgate, 0, 0).astype(BF16)
    back_gate = mm(dgate, wgate, 1, 1)
    dv, dvs, rim, last, dtraw, tap_grad, head_grad = kernel_call(
        back_body,
        (
            shape(count, width, BF16),
            shape(RIM + count, wide - width),
            shape(RIM, width),
            shape(RIM, width),
            shape(count, LANES, BF16),
            shape(8, wide),
            shape(8, LANES),
        ),
        [
            pltpu.VMEM((LANES, width), F32),
            pltpu.VMEM((count, wide), F32),
            pltpu.VMEM((count + RIM, LANES), F32),
            pltpu.VMEM((count + 2 * RIM, LANES), F32),
        ],
        act, delta, acc, traw, info, segrow, ahead, small["perhead"], spread,
        states, later, dy, raw, halo, small["taps"],
    )
    state = own_half(dvs) + swap(own_half(dvs, True), "head", 1)
    joined = chain_shift(jnp.concatenate([rim, state[:RIM]], axis=1), -1)
    state = state[RIM:] + jnp.pad(joined[:, width:], ((count - RIM, 0), (0, 0)))
    dv = lax.dynamic_update_slice_in_dim(
        dv, (last + joined[:, :width]).astype(BF16), count - RIM, 0
    )
    narrow = jnp.concatenate([dv, state.astype(BF16), dtraw], axis=1)
    x_grad = mm(normed, narrow, 0, 0).astype(BF16)
    back_normed = head_sum(back_gate + mm(narrow, wx, 1, 1))
    e = back_normed * small["norm_gain"]
    norm_grad = jnp.sum(back_normed * residual * root, axis=0)
    features = residual.shape[1]
    upstream = (
        upstream
        + root * e
        - residual * (root**3 * jnp.sum(e * residual, axis=-1, keepdims=True) / features)
    )
    return upstream, (x_grad, gate_w_grad, out_grad), (norm_grad, tap_grad, head_grad, gate_grad)


def pad_lanes(x, size):
    return jnp.pad(x, [(0, 0)] * (x.ndim - 1) + [(0, size - x.shape[-1])])


def pad_rows(x, size=8):
    return jnp.pad(x, ((0, size - x.shape[0]), (0, 0)))


def on_device(
    tokens, segments, cotangent, inner_proj, state_proj, step_proj, out_proj, norm_gain,
    mix_kernel, mix_bias, state_kernel, state_bias, step_bias, decay_log, skip_gain, gate_gain,
):
    layers = inner_proj.shape[0]
    features = tokens.shape[2]
    width = inner_proj.shape[3]
    heads = step_proj.shape[2]
    states = state_proj.shape[2]
    wide = width + states
    count = 2 * segments.shape[1]
    ctx, here = lax.axis_size("ctx"), lax.axis_index("ctx")
    me = lax.axis_index("dp") * ctx + here

    parts = []
    for layer in range(layers):
        parts.append(
            jnp.concatenate(
                [
                    inner_proj[layer, :, 1],
                    own_half(state_proj[layer]),
                    pad_lanes(step_proj[layer], LANES),
                ],
                axis=1,
            )
        )
        parts.append(jnp.concatenate([inner_proj[layer, :, 0], out_proj[layer].T], axis=1))
    gathered = []
    near = None
    for part in parts:
        if near is not None:
            part, near = lax.optimization_barrier((part, near))
            gathered.append(gather_far(near))
        near = gather_near(part)
    gathered.append(gather_far(near))
    weights = []
    for layer in range(layers):
        wx, rest = gathered[2 * layer : 2 * layer + 2]
        wstate = swap(wx[:, width : width + LANES], "head", 1)
        weights.append((wx, wstate, rest[:, :width], rest[:, width:]))

    block = features // (lax.axis_size("dp") * ctx)
    at = lax.broadcasted_iota(jnp.int32, (features, features), 0)
    to = lax.broadcasted_iota(jnp.int32, (features, features), 1)
    place = to // block
    owner = place // ctx * ctx
    steps = ctx.bit_length() - 1
    for k in range(steps):
        owner = owner + ((place >> k) & 1) * (1 << (steps - 1 - k))
    order = (at == (owner ^ me) * block + to % block).astype(BF16)

    def enter(blocks, extra=None):
        run = shared(to_runs, blocks, extra)
        run, extra = (run, None) if extra is None else run
        run = mm(run.reshape(count, features), order)
        return run if extra is None else (run, extra)

    def leave(run):
        run = mm(run.astype(BF16), order, 1, 1).astype(BF16)
        return shared(from_runs, run.reshape(2, count // 2, features))

    labels = jnp.zeros((2, 16, features), BF16)
    labels = labels.at[:, 0, : count // 2].set(segments.astype(BF16))
    residual, labels = enter(tokens, labels)
    seg = labels[:, 0, : count // 2].astype(F32).reshape(count)
    known = jnp.concatenate([chain_shift(seg[count - RIM :], 1), seg])
    chunked = seg.reshape(-1, CHUNK)
    chunk_before = known[RIM - 1 : RIM - 1 + count].reshape(-1, CHUNK)[:, :1]
    flags = [
        seg,
        known[RIM - 1 : -1] == seg,
        known[RIM - 2 : -2] == seg,
        known[RIM - 3 : -3] == seg,
        (chunked == chunk_before).reshape(-1),
        (chunked == chunked[:, -1:]).reshape(-1),
        seg == known[RIM - 1],
        seg == seg[-1],
    ]
    info = pad_lanes(jnp.stack([flag.astype(F32) for flag in flags], axis=1), LANES)
    segrow = jnp.broadcast_to(seg[None], (8, count))
    beyond = jnp.pad(known, (0, 3), constant_values=-1)
    ahead = pad_lanes(
        jnp.stack(
            [(beyond[d : d + count + RIM] == known).astype(F32) for d in range(4)], axis=1
        ),
        LANES,
    )
    at = lax.broadcasted_iota(jnp.int32, (LANES, width), 0)
    to = lax.broadcasted_iota(jnp.int32, (LANES, width), 1)
    spread = (at == to // (width // heads)).astype(BF16)
    common = (info, segrow, ahead, spread)

    gains = mm(norm_gain, order.astype(F32), precision=HIGH)
    smalls = []
    for layer in range(layers):
        taps = jnp.concatenate(
            [
                jnp.concatenate([mix_kernel[layer], state_kernel[layer]], axis=1),
                jnp.concatenate([mix_bias[layer], state_bias[layer]])[None],
            ]
        )
        perhead = jnp.stack([step_bias[layer], decay_log[layer], skip_gain[layer]])
        smalls.append(
            {
                "norm_gain": gains[layer],
                "taps": pad_rows(taps),
                "perhead": pad_rows(pad_lanes(perhead, LANES)),
                "gate_gain": jnp.broadcast_to(gate_gain[layer][None], (8, width)),
            }
        )

    saved = []
    for layer in range(layers):
        residual, kept = layer_forward(residual, weights[layer], smalls[layer], common)
        saved.append(kept)
        if layer == 0:
            cotangent, residual = lax.optimization_barrier((cotangent, residual))
            upstream = enter(cotangent)
    mixed = leave(residual)
    shards = [None] * layers
    others = [None] * layers
    for layer in reversed(range(layers)):
        upstream, matrices, (norm_grad, tap_grad, head_grad, gate_grad) = layer_backward(
            upstream, weights[layer], smalls[layer], common, saved[layer]
        )
        x_grad, gate_w_grad, out_grad = matrices
        shards[layer] = (scatter_rows(gate_w_grad, out_grad), scatter_rows(x_grad))
        norm_grad = mm(norm_grad[None], order.astype(F32), 1, 1, precision=HIGH)
        shared_taps = tap_grad[:, width:]
        shared_taps = shared_taps + swap(shared_taps, "head", 1)
        others[layer] = jnp.concatenate(
            [
                norm_grad.reshape(-1),
                gate_grad[0],
                tap_grad[:5, :width].reshape(-1),
                shared_taps[:5].reshape(-1),
                head_grad[:3].reshape(-1),
            ]
        ).reshape(-1, LANES)
    others = total_over(jnp.stack(others)).reshape(layers, -1)
    token_grad = leave(upstream)

    grads = [[], [], [], []]
    sums = [[] for _ in range(9)]
    for layer in range(layers):
        rest, x_shard = shards[layer]
        state_shard = x_shard[:, width : width + LANES]
        grads[0].append(jnp.stack([rest[:, :width], x_shard[:, :width]], axis=1))
        grads[1].append(both_halves(state_shard, swap(state_shard, "head", 1)))
        grads[2].append(x_shard[:, width + LANES : width + LANES + heads])
        grads[3].append(rest[:, width:].T)
        flat = others[layer]
        cut = 0
        pieces = []
        for size in (features, width, 5 * width, 5 * states, 3 * LANES):
            pieces.append(flat[cut : cut + size])
            cut += size
        taps = pieces[2].reshape(5, width)
        shared_taps = pieces[3].reshape(5, states)
        per = pieces[4].reshape(3, LANES)[:, :heads]
        for index, value in enumerate(
            (
                pieces[0], taps[:4], taps[4], shared_taps[:4], shared_taps[4],
                per[0], per[1], per[2], pieces[1],
            )
        ):
            sums[index].append(value)
    return (mixed, token_grad) + tuple(jnp.stack(v) for v in grads) + tuple(
        jnp.stack(v) for v in sums
    )


def solution(mesh):
    return jax.shard_map(
        on_device,
        mesh=mesh,
        in_specs=(
            P("dp", "ctx", None),
            P("dp", "ctx"),
            P("dp", "ctx", None),
            P(None, ("dp", "ctx"), None, "head"),
            P(None, ("dp", "ctx"), None),
            P(None, ("dp", "ctx"), "head"),
            P(None, "head", ("dp", "ctx")),
            P(),
            P(None, None, "head"),
            P(None, "head"),
            P(),
            P(),
            P(None, "head"),
            P(None, "head"),
            P(None, "head"),
            P(None, "head"),
        ),
        out_specs=(
            P("dp", "ctx", None),
            P("dp", "ctx", None),
            P(None, ("dp", "ctx"), None, "head"),
            P(None, ("dp", "ctx"), None),
            P(None, ("dp", "ctx"), "head"),
            P(None, "head", ("dp", "ctx")),
            P(),
            P(None, None, "head"),
            P(None, "head"),
            P(),
            P(),
            P(None, "head"),
            P(None, "head"),
            P(None, "head"),
            P(None, "head"),
        ),
        check_vma=False,
    )
```

```python
import jax
import jax.numpy as jnp
from jax import lax
from jax.experimental import pallas as pl
from jax.experimental.pallas import tpu as pltpu
from jax.sharding import PartitionSpec as P

EPSILON = 1e-05
F32 = jnp.float32
BF16 = jnp.bfloat16
HIGH = lax.Precision.HIGHEST
CHUNK = 128
LANES = 128
RIM = 8
FAR = -1e30


def mm(a, b, ca=1, cb=0, precision=None):
    return lax.dot_general(
        a, b, (((ca,), (cb,)), ((), ())), precision=precision, preferred_element_type=F32
    )


def split_mm(a, b, ca=1, cb=0):
    top = a.astype(BF16)
    rest = (a - top.astype(F32)).astype(BF16)
    return mm(top, b, ca, cb) + mm(rest, b, ca, cb)


def mm_split(a, b, ca=1, cb=0):
    top = b.astype(BF16)
    rest = (b - top.astype(F32)).astype(BF16)
    return mm(a, top, ca, cb) + mm(a, rest, ca, cb)


def kernel_call(body, outs, scratch, *args):
    return pl.pallas_call(
        body,
        out_shape=outs,
        scratch_shapes=scratch,
        compiler_params=pltpu.CompilerParams(vmem_limit_bytes=48 * 1024 * 1024),
    )(*args)


def grid_masks():
    row = lax.broadcasted_iota(jnp.int32, (CHUNK, CHUNK), 0)
    col = lax.broadcasted_iota(jnp.int32, (CHUNK, CHUNK), 1)
    return row, col


def soft(v):
    return jnp.maximum(v, 0.0) + jnp.log1p(jnp.exp(-jnp.abs(v)))


def sigmoid(v):
    return 1.0 / (1.0 + jnp.exp(-v))


def conv_body(
    raw_ref, halo_ref, traw_ref, info_ref, taps_ref, perhead_ref, spread_ref,
    act_ref, delta_ref, acc_ref, state_ref, total_ref, window,
):
    count, wide = raw_ref.shape
    chunks = count // CHUNK
    width = spread_ref.shape[1]
    row, col = grid_masks()
    tri = (row >= col).astype(F32)
    totals = []
    for c in range(chunks):
        rows = pl.ds(c * CHUNK, CHUNK)
        delta = soft(traw_ref[rows, :] + perhead_ref[0:1, :])
        rate = -delta * jnp.exp(perhead_ref[1:2, :])
        acc = mm(tri, rate, precision=HIGH)
        delta_ref[rows, :] = delta
        acc_ref[rows, :] = acc
        totals.append(acc[CHUNK - 1 : CHUNK, :])
    whole = totals[0]
    for c in range(1, chunks):
        whole = whole + totals[c]
    total_ref[...] = jnp.broadcast_to(
        jnp.exp(whole) * info_ref[count - 1 : count, 6:7], total_ref.shape
    )

    def block(cb, _):
        lanes = pl.ds(pl.multiple_of(cb * LANES, LANES), LANES)
        window[0:RIM, :] = halo_ref[:, lanes].astype(F32)
        window[RIM : RIM + count, :] = raw_ref[:, lanes].astype(F32)
        taps = taps_ref[:, lanes]
        for c in range(chunks):
            base = c * CHUNK
            pre = taps[4:5, :] + taps[3:4, :] * window[RIM + base : RIM + base + CHUNK, :]
            for d in (1, 2, 3):
                moved = window[RIM + base - d : RIM + base - d + CHUNK, :]
                pre = pre + taps[3 - d : 4 - d, :] * (
                    moved * info_ref[base : base + CHUNK, d : d + 1]
                )
            act_ref[base : base + CHUNK, lanes] = (pre * sigmoid(pre)).astype(BF16)
        return 0

    lax.fori_loop(0, wide // LANES, block, 0)
    spread = spread_ref[...]
    state = jnp.zeros((LANES, width), F32)
    after = jnp.zeros_like(totals[0])
    for c in reversed(range(chunks)):
        rows = pl.ds(c * CHUNK, CHUNK)
        weight = (
            jnp.exp(totals[c] - acc_ref[rows, :] + after) * info_ref[rows, 7:8] * delta_ref[rows, :]
        )
        scaled = act_ref[rows, 0:width].astype(F32) * split_mm(weight, spread)
        state = state + mm_split(act_ref[rows, width : width + LANES], scaled, 0, 0)
        after = after + totals[c]
    state_ref[...] = state


def chunk_terms(c, acc_ref, info_ref, segrow_ref):
    rows = pl.ds(pl.multiple_of(c * CHUNK, CHUNK), CHUNK)
    acc = acc_ref[rows, :]
    row, col = grid_masks()
    same = (info_ref[rows, 0:1] == segrow_ref[0:1, rows]) & (row >= col)
    blocked = jnp.where(same, 0.0, FAR)
    total = acc[CHUNK - 1 : CHUNK, :]
    flags = info_ref[rows, :]
    entry = jnp.exp(acc) * flags[:, 4:5]
    tail = jnp.exp(total - acc) * flags[:, 5:6]
    carry = jnp.exp(total) * flags[CHUNK - 1 : CHUNK, 4:5]
    return rows, acc, acc.T, blocked, entry, tail, carry


def mix_body(
    act_ref, delta_ref, acc_ref, info_ref, segrow_ref, perhead_ref, spread_ref, start_ref,
    gate_ref, gain_ref, y_ref, scaled_ref, squares_ref, states_ref, state,
):
    count, width = gate_ref.shape
    spread = spread_ref[...]
    state[...] = start_ref[...].astype(F32)
    skip = split_mm(perhead_ref[...], spread)[2:3, :]
    lane = lax.broadcasted_iota(jnp.int32, (CHUNK, LANES), 1)
    low_half = lane < LANES // 2

    def step(c, _):
        rows, acc, across, blocked, entry, tail, carry = chunk_terms(
            c, acc_ref, info_ref, segrow_ref
        )
        now = state[...]
        now_low = now.astype(BF16)
        states_ref[pl.ds(pl.multiple_of(c * LANES, LANES), LANES), :] = now_low
        bstate = act_ref[rows, width : width + LANES]
        cstate = act_ref[rows, width + LANES : width + 2 * LANES]
        gram = mm(cstate, bstate, 1, 1)
        x = act_ref[rows, 0:width].astype(F32)
        scaled = x * split_mm(delta_ref[rows, :], spread)
        z = scaled.astype(BF16)
        y_ref[rows, :] = split_mm(entry, spread) * mm_split(cstate, now) + skip * x
        tailed = scaled * split_mm(tail, spread)
        state[...] = split_mm(carry, spread) * now + mm_split(bstate, tailed, 0, 0)
        squares = jnp.zeros((CHUNK, LANES), F32)
        for pair in range(width // LANES):
            lanes = slice(pair * LANES, (pair + 1) * LANES)
            zb = z[:, lanes]
            out = y_ref[rows, lanes]
            for half in (0, 1):
                h = 2 * pair + half
                decay = jnp.exp(acc[:, h : h + 1] - across[h : h + 1, :] + blocked)
                keep = low_half if half == 0 else jnp.logical_not(low_half)
                zh = jnp.where(keep, zb, jnp.zeros_like(zb))
                zl = (jnp.where(keep, scaled[:, lanes], 0.0) - zh.astype(F32)).astype(BF16)
                mat = gram * decay
                top = mat.astype(BF16)
                rest = (mat - top.astype(F32)).astype(BF16)
                out = out + mm(top, zh) + mm(rest, zh) + mm(top, zl)
            y_ref[rows, lanes] = out
            gate = gate_ref[rows, lanes]
            gated = out * (gate * sigmoid(gate))
            squares = squares + gated * gated
            scaled_ref[rows, lanes] = gated
        squares_ref[rows, :] = jnp.broadcast_to(
            jnp.sum(squares, axis=1, keepdims=True), (CHUNK, LANES)
        )
        return 0

    lax.fori_loop(0, count // CHUNK, step, 0)


def gate_body(
    bn_ref, y_ref, gate_ref, gain_ref, factor_ref, act_ref, acc_ref, info_ref, spread_ref,
    dy_ref, dgate_ref, ggrad_ref, state_ref,
):
    count, width = bn_ref.shape
    chunks = count // CHUNK
    spread = spread_ref[...]
    state = jnp.zeros((LANES, width), F32)
    before = jnp.zeros((1, LANES), F32)
    sums = jnp.zeros((1, width), F32)
    for c in range(chunks):
        rows = slice(c * CHUNK, (c + 1) * CHUNK)
        bn = bn_ref[rows, :]
        y = y_ref[rows, :]
        gate = gate_ref[rows, :]
        root = factor_ref[rows, 0:1]
        coef = factor_ref[rows, 1:2]
        sig = sigmoid(gate)
        silu = gate * sig
        gated = y * silu
        back = root * (bn * gain_ref[0:1, :]) - gated * coef
        dy = back * silu
        dy_ref[rows, :] = dy.astype(BF16)
        dgate_ref[rows, :] = (back * y * (sig * (1.0 + gate * (1.0 - sig)))).astype(BF16)
        sums = sums + jnp.sum(bn * gated * root, axis=0, keepdims=True)
        acc = acc_ref[rows, :]
        entry = jnp.exp(acc + before) * info_ref[rows, 6:7]
        cstate = act_ref[rows, width + LANES : width + 2 * LANES]
        state = state + mm(cstate, (dy * split_mm(entry, spread)).astype(BF16), 0, 0)
        before = before + acc[CHUNK - 1 : CHUNK, :]
    ggrad_ref[...] = jnp.broadcast_to(sums, ggrad_ref.shape)
    state_ref[...] = state.astype(BF16)


def back_body(
    act_ref, delta_ref, acc_ref, traw_ref, info_ref, segrow_ref, ahead_ref, perhead_ref, spread_ref,
    states_ref, later_ref, dy_ref, raw_ref, halo_ref, taps_ref,
    dv_ref, dvs_ref, rim_ref, last_ref, dtraw_ref, tapgrad_ref, headgrad_ref,
    dstate, dact, window, gradient,
):
    count, wide = raw_ref.shape
    width = spread_ref.shape[1]
    chunks = count // CHUNK
    spread = spread_ref[...]
    dstate[...] = later_ref[...].astype(F32)
    skip = split_mm(perhead_ref[...], spread)[2:3, :]
    row, col = grid_masks()
    upper = (row <= col).astype(F32)
    lower = (row > col).astype(F32)
    upper_low = upper.astype(BF16)
    lane = lax.broadcasted_iota(jnp.int32, (CHUNK, LANES), 1)
    low_half = lane < LANES // 2
    headgrad_ref[...] = jnp.zeros_like(headgrad_ref)
    decay_rate = jnp.exp(perhead_ref[1:2, :])

    def step(index, _):
        c = chunks - 1 - index
        rows, acc, across, blocked, entry, tail, carry = chunk_terms(
            c, acc_ref, info_ref, segrow_ref
        )
        delta = delta_ref[rows, :]
        bstate = act_ref[rows, width : width + LANES]
        cstate = act_ref[rows, width + LANES : width + 2 * LANES]
        gram = mm(cstate, bstate, 1, 1)
        x = act_ref[rows, 0:width].astype(F32)
        dy_low = dy_ref[rows, :]
        dy = dy_low.astype(F32)
        wide_delta = split_mm(delta, spread)
        scaled = x * wide_delta
        z = scaled.astype(BF16)
        later = dstate[...]
        later_low = later.astype(BF16)
        now_low = states_ref[pl.ds(pl.multiple_of(c * LANES, LANES), LANES), :]
        wide_tail = split_mm(tail, spread)
        tail_in = wide_tail * mm(bstate, later_low)
        entered = dy * split_mm(entry, spread)
        entered_low = entered.astype(BF16)
        from_entry = split_mm(entered * mm(cstate, now_low), spread, 1, 1)
        from_tail = split_mm(scaled * tail_in, spread, 1, 1)
        wide_carry = split_mm(carry, spread)
        kept = jnp.sum(later * now_low.astype(F32), axis=0, keepdims=True) * wide_carry
        from_carry = split_mm(jnp.broadcast_to(kept, (8, width)), spread, 1, 1)[0:1, :]
        dstate[...] = wide_carry * later + mm(cstate, entered_low, 0, 0)
        drate = (
            mm(upper, from_entry, precision=HIGH) + mm(lower, from_tail, precision=HIGH) + from_carry
        )
        dgram = jnp.zeros((CHUNK, CHUNK), F32)
        direct = jnp.zeros((CHUNK, LANES), F32)
        for pair in range(width // LANES):
            lanes = slice(pair * LANES, (pair + 1) * LANES)
            zb = z[:, lanes]
            dyb = dy_low[:, lanes]
            back = tail_in[:, lanes]
            for half in (0, 1):
                h = 2 * pair + half
                keep = low_half if half == 0 else jnp.logical_not(low_half)
                dyh = jnp.where(keep, dyb, jnp.zeros_like(dyb))
                decay = jnp.exp(acc[:, h : h + 1] - across[h : h + 1, :] + blocked)
                grad = mm(dyh, zb, 1, 1) * decay
                dgram = dgram + grad
                moved = mm(upper_low, (grad * gram).astype(BF16)) * lower
                drate = drate + jnp.where(lane == h, jnp.sum(moved, axis=1, keepdims=True), 0.0)
                back = back + mm((gram * decay).astype(BF16), dyh, 0, 0)
            direct = direct + split_mm(x[:, lanes] * back, spread[:, lanes], 1, 1)
            dact[rows, lanes] = wide_delta[:, lanes] * back + skip[:, lanes] * dy[:, lanes]
        dgram_low = dgram.astype(BF16)
        tailed = (scaled * wide_tail).astype(BF16)
        dact[rows, width : width + LANES] = mm(dgram_low, cstate, 0, 0) + mm(
            tailed, later_low, 1, 1
        )
        dact[rows, width + LANES : width + 2 * LANES] = mm(dgram_low, bstate) + mm(
            entered_low, now_low, 1, 1
        )
        ddelta = direct - decay_rate * drate
        dtraw = ddelta * sigmoid(traw_ref[rows, :] + perhead_ref[0:1, :])
        dtraw_ref[rows, :] = dtraw.astype(BF16)
        rate = -delta * decay_rate
        skipped = split_mm(x * dy, spread, 1, 1)
        headgrad_ref[0:1, :] += jnp.sum(dtraw, axis=0, keepdims=True)
        headgrad_ref[1:2, :] += jnp.sum(drate * rate, axis=0, keepdims=True)
        headgrad_ref[2:3, :] += jnp.sum(skipped, axis=0, keepdims=True)
        return 0

    lax.fori_loop(0, chunks, step, 0)
    gradient[0:RIM, :] = jnp.zeros((RIM, LANES), F32)
    gradient[RIM + count : 2 * RIM + count, :] = jnp.zeros((RIM, LANES), F32)

    def block(lanes, put):
        window[0:RIM, :] = halo_ref[:, lanes].astype(F32)
        window[RIM : RIM + count, :] = raw_ref[:, lanes].astype(F32)
        taps = taps_ref[:, lanes]
        sums = [jnp.zeros((1, LANES), F32) for _ in range(5)]
        for c in range(chunks):
            base = c * CHUNK
            moved = [window[RIM + base : RIM + base + CHUNK, :]]
            for d in (1, 2, 3):
                moved.append(
                    window[RIM + base - d : RIM + base - d + CHUNK, :]
                    * info_ref[base : base + CHUNK, d : d + 1]
                )
            pre = taps[4:5, :]
            for d in range(4):
                pre = pre + taps[3 - d : 4 - d, :] * moved[d]
            sig = sigmoid(pre)
            dpre = dact[base : base + CHUNK, lanes] * (sig * (1.0 + pre * (1.0 - sig)))
            gradient[RIM + base : RIM + base + CHUNK, :] = dpre
            for d in range(4):
                sums[3 - d] = sums[3 - d] + jnp.sum(dpre * moved[d], axis=0, keepdims=True)
            sums[4] = sums[4] + jnp.sum(dpre, axis=0, keepdims=True)
        for index in range(5):
            tapgrad_ref[index : index + 1, lanes] = sums[index]

        def pulled(base, size):
            out = taps[3:4, :] * gradient[base : base + size, :]
            for d in (1, 2, 3):
                out = out + taps[3 - d : 4 - d, :] * (
                    gradient[base + d : base + d + size, :] * ahead_ref[base : base + size, d : d + 1]
                )
            return out

        put(pulled, lanes)

    def put_x(pulled, lanes):
        rim_ref[:, lanes] = pulled(0, RIM)
        for c in range(chunks):
            back = pulled(RIM + c * CHUNK, CHUNK)
            dv_ref[c * CHUNK : (c + 1) * CHUNK, lanes] = back.astype(BF16)
            if c == chunks - 1:
                last_ref[:, lanes] = back[CHUNK - RIM :, :]

    def put_state(at):
        def put(pulled, lanes):
            dvs_ref[0:RIM, at : at + LANES] = pulled(0, RIM)
            for c in range(chunks):
                base = RIM + c * CHUNK
                dvs_ref[base : base + CHUNK, at : at + LANES] = pulled(base, CHUNK)

        return put

    def loop(cb, _):
        block(pl.ds(pl.multiple_of(cb * LANES, LANES), LANES), put_x)
        return 0

    lax.fori_loop(0, width // LANES, loop, 0)
    for at in range(0, wide - width, LANES):
        block(slice(width + at, width + at + LANES), put_state(at))
    tapgrad_ref[5:8, :] = jnp.zeros((3, wide), F32)


def swap(x, axis, bit):
    size = lax.axis_size(axis)
    return lax.ppermute(x, axis, [(i, i ^ bit) for i in range(size)])


def bits_of(axis):
    size = lax.axis_size(axis)
    return [1 << k for k in reversed(range(size.bit_length() - 1))]


def after(value, *ties):
    ties = [tie for tie in ties if tie is not None]
    return lax.optimization_barrier((value, ties))[0] if ties else value


def gather_all(parts, follow):
    wholes = []
    four = lax.axis_size("dp") == 4
    near_before = cross_before = None
    for index, part in enumerate(parts):
        near = after(part, near_before)
        for bit in bits_of("ctx"):
            near = jnp.concatenate([near, swap(near, "ctx", bit)], axis=0)
        if index == 0:
            follow(near)
        near_before = near
        near = after(near, cross_before)
        if not four:
            for bit in reversed(bits_of("dp")):
                near = jnp.concatenate([near, swap(near, "dp", bit)], axis=0)
            cross_before = near
            wholes.append(near)
            continue
        half = near.shape[0] // 2
        one = swap(near, "dp", 1)
        two = swap(near, "dp", 2)
        three = [swap(one[:half], "dp", 2), swap(two[half:], "dp", 1)]
        cross_before = three if index % 2 == 0 and index > 0 else (one, two)
        wholes.append(jnp.concatenate([near, one, two] + three, axis=0))
    return wholes


def scatter_steps(*matrices):
    count = lax.axis_size("dp")
    group = matrices[0].shape[0] // count

    def part(start, size):
        return jnp.concatenate([g[start : start + size] for g in matrices], axis=1)

    if count != 4:
        near = part(0, count * group).astype(F32)
        for bit in bits_of("dp"):
            size = bit * group
            got = swap(near[size:].astype(BF16), "dp", bit)
            got = yield got
            near = near[:size] + got.astype(F32)
    else:
        half = group // 2
        far = (
            swap(part(3 * group, half), "dp", 2),
            swap(part(3 * group + half, half), "dp", 1),
        )
        far = yield far
        none = jnp.zeros(far[0].shape, F32)
        one = part(group, group).astype(F32) + jnp.concatenate([far[0].astype(F32), none])
        two = part(2 * group, group).astype(F32) + jnp.concatenate([none, far[1].astype(F32)])
        got = (swap(one.astype(BF16), "dp", 1), swap(two.astype(BF16), "dp", 2))
        got = yield got
        near = part(0, group).astype(F32) + got[0].astype(F32) + got[1].astype(F32)
    for bit in reversed(bits_of("ctx")):
        half = near.shape[0] // 2
        got = swap(near[half:].astype(BF16), "ctx", bit)
        got = yield got
        near = near[:half] + got.astype(F32)
    return near


class Scatter:
    def __init__(self, steps):
        self.steps = steps
        self.result = None
        self.flying = next(self.steps)

    def step(self, got):
        try:
            self.flying = self.steps.send(got)
        except StopIteration as stop:
            self.result = stop.value


def advance(scatters, value):
    scatters = [scatter for scatter in scatters if scatter.result is None]
    if scatters:
        flying = [scatter.flying for scatter in scatters]
        value, flying = lax.optimization_barrier((value, flying))
        for scatter, got in zip(scatters, flying):
            scatter.step(got)
    return value


def total_steps(x):
    for axis in ("dp", "ctx"):
        for bit in reversed(bits_of(axis)):
            got = yield swap(x, axis, bit)
            x = x + got
    return x


def head_sum(x):
    low = x.astype(BF16)
    return low.astype(F32) + swap(low, "head", 1).astype(F32)


def own_half(x, other=False):
    half = x.shape[-1] // 2
    first = (lax.axis_index("head") == 0) != other
    return jnp.where(first, x[..., :half], x[..., half:])


def both_halves(own, other):
    return jnp.where(
        lax.axis_index("head") == 0,
        jnp.concatenate([own, other], axis=-1),
        jnp.concatenate([other, own], axis=-1),
    )


def to_runs(blocks):
    count, me = lax.axis_size("ctx"), lax.axis_index("ctx")
    even = me % 2 == 0
    first = jnp.where(even, blocks[0], blocks[1])
    second = jnp.where(even, blocks[1], blocks[0])
    half = count // 2
    one = [(2 * j, j) for j in range(half)] + [(2 * j + 1, half + j) for j in range(half)]
    two = [(2 * j + 1, j) for j in range(half)] + [(2 * j, half + j) for j in range(half)]
    got_one = lax.ppermute(first, "ctx", one)
    got_two = lax.ppermute(second, "ctx", two)
    early = me < half
    return jnp.stack([jnp.where(early, got_one, got_two), jnp.where(early, got_two, got_one)])


def from_runs(blocks):
    count, me = lax.axis_size("ctx"), lax.axis_index("ctx")
    half = count // 2
    early = me < half
    one = [(j, 2 * j) for j in range(half)] + [(half + j, 2 * j + 1) for j in range(half)]
    two = [(j, 2 * j + 1) for j in range(half)] + [(half + j, 2 * j) for j in range(half)]
    got_one = lax.ppermute(jnp.where(early, blocks[0], blocks[1]), "ctx", one)
    got_two = lax.ppermute(jnp.where(early, blocks[1], blocks[0]), "ctx", two)
    even = me % 2 == 0
    return jnp.stack([jnp.where(even, got_one, got_two), jnp.where(even, got_two, got_one)])


def shared(move, blocks, extra=None):
    rows = blocks.shape[1] // 2
    mine = lax.axis_index("head")
    send = lax.dynamic_slice_in_dim(blocks, mine * rows, rows, 1)
    if extra is not None:
        send = jnp.concatenate([send, extra], axis=1)
    got = move(send)
    own = got[:, :rows]
    other = swap(own, "head", 1)
    whole = jnp.where(
        mine == 0,
        jnp.concatenate([own, other], axis=1),
        jnp.concatenate([other, own], axis=1),
    )
    return whole if extra is None else (whole, got[:, rows:])


def chain_shift(x, by):
    count = lax.axis_size("ctx")
    half = count // 2
    pairs = [
        (i, i + by) for i in range(count) if 0 <= i + by < count and i // half == (i + by) // half
    ]
    return lax.ppermute(x, "ctx", pairs)


def chain_scan(state, total, back):
    sign = -1 if back else 1
    half = lax.axis_size("ctx") // 2
    state = chain_shift(state, sign)
    if half == 2:
        return state
    total = chain_shift(total, sign)
    state = state.astype(F32)
    by = 1
    while by < half - 1:
        state = state + total * chain_shift(state, sign * by)
        total = total * chain_shift(total, sign * by)
        by *= 2
    return state.astype(BF16)


def shape(rows, cols, kind=F32):
    return jax.ShapeDtypeStruct((rows, cols), kind)


def layer_forward(residual, weights, small, common):
    wx, wstate, wgate, wout = weights
    info, segrow, _, spread = common
    count = residual.shape[0]
    width = spread.shape[1]
    wide = width + 2 * LANES
    root = lax.rsqrt(jnp.mean(residual * residual, axis=-1, keepdims=True) + EPSILON)
    normed = (residual * root * small["norm_gain"]).astype(BF16)
    both = mm(normed, wx)
    sraw = both_halves(both[:, width : width + LANES], mm(normed, wstate)).astype(BF16)
    raw = jnp.concatenate([both[:, :width].astype(BF16), sraw], axis=1)
    traw = both[:, width + LANES :]
    halo = chain_shift(raw[count - RIM :], 1)
    gate = mm(normed, wgate)
    act, delta, acc, state, total = kernel_call(
        conv_body,
        (
            shape(count, wide, BF16),
            shape(count, LANES),
            shape(count, LANES),
            shape(LANES, width),
            shape(8, LANES),
        ),
        [pltpu.VMEM((count + RIM, LANES), F32)],
        raw, halo, traw, info, small["taps"], small["perhead"], spread,
    )
    wide_total = jnp.repeat(total[0:1, : width // 64], 64, axis=1)
    start = chain_scan(state, wide_total, False)
    y, gated, squares, states = kernel_call(
        mix_body,
        (
            shape(count, width),
            shape(count, width),
            shape(count, LANES),
            shape(count, width, BF16),
        ),
        [pltpu.VMEM((LANES, width), F32)],
        act, delta, acc, info, segrow, small["perhead"], spread, start, gate, small["gate_gain"],
    )
    own = squares[:, 0:1]
    channels = width * lax.axis_size("head")
    out_root = lax.rsqrt((own + swap(own, "head", 1)) / channels + EPSILON)
    normal = (gated * out_root * small["gate_gain"][0:1]).astype(BF16)
    branch = mm(normal, wout, 1, 1)
    branch = branch + swap(branch, "head", 1)
    kept = (residual, root, normed, raw, traw, halo, gate, act, delta, acc, wide_total, y, normal)
    return residual + branch, kept + (states, out_root, branch)


def layer_backward(upstream, weights, small, common, kept, pending):
    wx, _, wgate, wout = weights
    info, segrow, ahead, spread = common
    (
        residual, root, normed, raw, traw, halo, gate, act, delta, acc, wide_total, y, normal,
        states, out_root, branch,
    ) = kept
    count = residual.shape[0]
    width = spread.shape[1]
    wide = width + 2 * LANES
    channels = width * lax.axis_size("head")
    wire = upstream.astype(BF16)
    bn = mm(wire, wout)
    dot = jnp.sum(wire.astype(F32) * branch, axis=-1, keepdims=True)
    factor = jnp.concatenate(
        [out_root, out_root**2 * dot / channels, jnp.zeros((count, LANES - 2), F32)], axis=1
    )
    dy, dgate, gate_grad, local = kernel_call(
        gate_body,
        (
            shape(count, width, BF16),
            shape(count, width, BF16),
            shape(8, width),
            shape(LANES, width, BF16),
        ),
        [],
        bn, y, gate, small["gate_gain"], factor, act, acc, info, spread,
    )
    later = chain_scan(local, wide_total, True)
    out_grad = mm(wire, normal, 0, 0).astype(BF16)
    gate_w_grad = mm(normed, dgate, 0, 0).astype(BF16)
    later = advance(pending, later)
    rest = Scatter(scatter_steps(gate_w_grad, out_grad))
    back_gate = mm(dgate, wgate, 1, 1)
    dv, dvs, rim, last, dtraw, tap_grad, head_grad = kernel_call(
        back_body,
        (
            shape(count, width, BF16),
            shape(RIM + count, wide - width),
            shape(RIM, width),
            shape(RIM, width),
            shape(count, LANES, BF16),
            shape(8, wide),
            shape(8, LANES),
        ),
        [
            pltpu.VMEM((LANES, width), F32),
            pltpu.VMEM((count, wide), F32),
            pltpu.VMEM((count + RIM, LANES), F32),
            pltpu.VMEM((count + 2 * RIM, LANES), F32),
        ],
        act, delta, acc, traw, info, segrow, ahead, small["perhead"], spread,
        states, later, dy, raw, halo, small["taps"],
    )
    state = own_half(dvs) + swap(own_half(dvs, True), "head", 1)
    joined = chain_shift(jnp.concatenate([rim, state[:RIM]], axis=1), -1)
    state = state[RIM:] + jnp.pad(joined[:, width:], ((count - RIM, 0), (0, 0)))
    dv = lax.dynamic_update_slice_in_dim(
        dv, (last + joined[:, :width]).astype(BF16), count - RIM, 0
    )
    narrow = jnp.concatenate([dv, state.astype(BF16), dtraw], axis=1)
    narrow = advance(pending + [rest], narrow)
    x_grad = mm(normed, narrow, 0, 0).astype(BF16)
    pending = pending + [rest, Scatter(scatter_steps(x_grad))]
    back_normed = head_sum(back_gate + mm(narrow, wx, 1, 1))
    e = back_normed * small["norm_gain"]
    norm_grad = jnp.sum(back_normed * residual * root, axis=0)
    features = residual.shape[1]
    upstream = (
        upstream
        + root * e
        - residual * (root**3 * jnp.sum(e * residual, axis=-1, keepdims=True) / features)
    )
    return upstream, pending, (norm_grad, tap_grad, head_grad, gate_grad)


def pad_lanes(x, size):
    return jnp.pad(x, [(0, 0)] * (x.ndim - 1) + [(0, size - x.shape[-1])])


def pad_rows(x, size=8):
    return jnp.pad(x, ((0, size - x.shape[0]), (0, 0)))


def on_device(
    tokens, segments, cotangent, inner_proj, state_proj, step_proj, out_proj, norm_gain,
    mix_kernel, mix_bias, state_kernel, state_bias, step_bias, decay_log, skip_gain, gate_gain,
):
    layers = inner_proj.shape[0]
    features = tokens.shape[2]
    width = inner_proj.shape[3]
    heads = step_proj.shape[2]
    states = state_proj.shape[2]
    wide = width + states
    count = 2 * segments.shape[1]
    ctx, here = lax.axis_size("ctx"), lax.axis_index("ctx")
    me = lax.axis_index("dp") * ctx + here

    parts = []
    for layer in range(layers):
        first = [
            inner_proj[layer, :, 1],
            own_half(state_proj[layer]),
            pad_lanes(step_proj[layer], LANES),
        ]
        rest = [inner_proj[layer, :, 0], out_proj[layer].T]
        parts.extend(jnp.concatenate(group, axis=1) for group in (first, rest))
    began = []
    gathered = gather_all(parts, began.append)
    weights = []
    for layer in range(layers):
        wx, rest = gathered[2 * layer : 2 * layer + 2]
        wstate = swap(wx[:, width : width + LANES], "head", 1)
        weights.append((wx, wstate, rest[:, :width], rest[:, width:]))

    block = features // (lax.axis_size("dp") * ctx)
    at = lax.broadcasted_iota(jnp.int32, (features, features), 0)
    to = lax.broadcasted_iota(jnp.int32, (features, features), 1)
    place = to // block
    owner = place // ctx * ctx
    steps = ctx.bit_length() - 1
    for k in range(steps):
        owner = owner + ((place >> k) & 1) * (1 << (steps - 1 - k))
    order = (at == (owner ^ me) * block + to % block).astype(BF16)

    def enter(blocks, extra=None):
        run = shared(to_runs, blocks, extra)
        run, extra = (run, None) if extra is None else run
        run = mm(run.reshape(count, features), order)
        return run if extra is None else (run, extra)

    def leave(run):
        run = mm(run.astype(BF16), order, 1, 1).astype(BF16)
        return shared(from_runs, run.reshape(2, count // 2, features))

    rows = count // 2
    behind = [(i, i + 1) for i in range(ctx - 1)]
    previous = lax.ppermute(after(segments, *began)[:, rows - RIM :], "ctx", behind)
    labels = jnp.concatenate([segments, previous], axis=1).astype(BF16)
    labels = jnp.pad(labels[:, None], ((0, 0), (0, 15), (0, features - rows - RIM)))
    residual, labels = enter(after(tokens, *began), labels)
    labels = labels[:, 0].astype(F32)
    seg = labels[:, :rows].reshape(count)
    known = jnp.concatenate([labels[0, rows : rows + RIM], seg])
    chunked = seg.reshape(-1, CHUNK)
    chunk_before = known[RIM - 1 : RIM - 1 + count].reshape(-1, CHUNK)[:, :1]
    flags = [
        seg,
        known[RIM - 1 : -1] == seg,
        known[RIM - 2 : -2] == seg,
        known[RIM - 3 : -3] == seg,
        (chunked == chunk_before).reshape(-1),
        (chunked == chunked[:, -1:]).reshape(-1),
        seg == known[RIM - 1],
        seg == seg[-1],
    ]
    info = pad_lanes(jnp.stack([flag.astype(F32) for flag in flags], axis=1), LANES)
    segrow = jnp.broadcast_to(seg[None], (8, count))
    beyond = jnp.pad(known, (0, 3), constant_values=-1)
    ahead = pad_lanes(
        jnp.stack(
            [(beyond[d : d + count + RIM] == known).astype(F32) for d in range(4)], axis=1
        ),
        LANES,
    )
    at = lax.broadcasted_iota(jnp.int32, (LANES, width), 0)
    to = lax.broadcasted_iota(jnp.int32, (LANES, width), 1)
    spread = (at == to // (width // heads)).astype(BF16)
    common = (info, segrow, ahead, spread)

    gains = mm(norm_gain, order.astype(F32), precision=HIGH)
    smalls = []
    for layer in range(layers):
        taps = jnp.concatenate(
            [
                jnp.concatenate([mix_kernel[layer], state_kernel[layer]], axis=1),
                jnp.concatenate([mix_bias[layer], state_bias[layer]])[None],
            ]
        )
        perhead = jnp.stack([step_bias[layer], decay_log[layer], skip_gain[layer]])
        smalls.append(
            {
                "norm_gain": gains[layer],
                "taps": pad_rows(taps),
                "perhead": pad_rows(pad_lanes(perhead, LANES)),
                "gate_gain": jnp.broadcast_to(gate_gain[layer][None], (8, width)),
            }
        )

    saved = []
    for layer in range(layers):
        residual, kept = layer_forward(residual, weights[layer], smalls[layer], common)
        saved.append(kept)
        if layer == 0:
            cotangent = after(cotangent, gathered[0])
            upstream = enter(cotangent)
            residual, upstream = lax.optimization_barrier((residual, upstream))
    mixed = leave(residual)
    pending = []
    others = [None] * layers
    for layer in reversed(range(layers)):
        upstream, pending, (norm_grad, tap_grad, head_grad, gate_grad) = layer_backward(
            upstream, weights[layer], smalls[layer], common, saved[layer], pending
        )
        norm_grad = mm(norm_grad[None], order.astype(F32), 1, 1, precision=HIGH)
        shared_taps = tap_grad[:, width:]
        shared_taps = shared_taps + swap(shared_taps, "head", 1)
        others[layer] = jnp.concatenate(
            [
                norm_grad.reshape(-1),
                gate_grad[0],
                tap_grad[:5, :width].reshape(-1),
                shared_taps[:5].reshape(-1),
                head_grad[:3].reshape(-1),
            ]
        ).reshape(-1, LANES)
    pending.append(Scatter(total_steps(jnp.stack(others))))
    token_grad = leave(upstream)
    while any(scatter.result is None for scatter in pending):
        advance(pending, ())
    done = [scatter.result for scatter in pending]
    others = done.pop().reshape(layers, -1)
    shards = [done[2 * index : 2 * index + 2] for index in reversed(range(layers))]

    grads = [[], [], [], []]
    sums = [[] for _ in range(9)]
    for layer in range(layers):
        rest, x_shard = shards[layer]
        state_shard = x_shard[:, width : width + LANES]
        grads[0].append(jnp.stack([rest[:, :width], x_shard[:, :width]], axis=1))
        grads[1].append(both_halves(state_shard, swap(state_shard, "head", 1)))
        grads[2].append(x_shard[:, width + LANES : width + LANES + heads])
        grads[3].append(rest[:, width:].T)
        flat = others[layer]
        cut = 0
        pieces = []
        for size in (features, width, 5 * width, 5 * states, 3 * LANES):
            pieces.append(flat[cut : cut + size])
            cut += size
        taps = pieces[2].reshape(5, width)
        shared_taps = pieces[3].reshape(5, states)
        per = pieces[4].reshape(3, LANES)[:, :heads]
        for index, value in enumerate(
            (
                pieces[0], taps[:4], taps[4], shared_taps[:4], shared_taps[4],
                per[0], per[1], per[2], pieces[1],
            )
        ):
            sums[index].append(value)
    return (mixed, token_grad) + tuple(jnp.stack(v) for v in grads) + tuple(
        jnp.stack(v) for v in sums
    )


def solution(mesh):
    return jax.shard_map(
        on_device,
        mesh=mesh,
        in_specs=(
            P("dp", "ctx", None),
            P("dp", "ctx"),
            P("dp", "ctx", None),
            P(None, ("dp", "ctx"), None, "head"),
            P(None, ("dp", "ctx"), None),
            P(None, ("dp", "ctx"), "head"),
            P(None, "head", ("dp", "ctx")),
            P(),
            P(None, None, "head"),
            P(None, "head"),
            P(),
            P(),
            P(None, "head"),
            P(None, "head"),
            P(None, "head"),
            P(None, "head"),
        ),
        out_specs=(
            P("dp", "ctx", None),
            P("dp", "ctx", None),
            P(None, ("dp", "ctx"), None, "head"),
            P(None, ("dp", "ctx"), None),
            P(None, ("dp", "ctx"), "head"),
            P(None, "head", ("dp", "ctx")),
            P(),
            P(None, None, "head"),
            P(None, "head"),
            P(),
            P(),
            P(None, "head"),
            P(None, "head"),
            P(None, "head"),
            P(None, "head"),
        ),
        check_vma=False,
    )
```
